32 devices in a mesh: ctx: 8 (over y, x, core), dp: 4 (over z).
Axes of the slice: x: 2, y: 2, z: 4, core: 2. Of those that a mesh axis runs over, the one named last changes fastest.
Arguments:
- query_in: bfloat16 [4096, 8192], P('ctx', 'dp'), may hold values from -6 to 6
- key_in: bfloat16 [4096, 8192], P('ctx', 'dp'), may hold values from -6 to 6
- value_in: bfloat16 [4096, 8192], P('ctx', 'dp'), may hold values from -280 to 280
- log_decay: float32 [64, 4096], P('dp', 'ctx'), may hold values from -0.8 to 0
- norm_gain: float32 [8192], P('dp'), may hold values from 0.25 to 1.75
- grad_out: bfloat16 [4096, 8192], P('ctx', 'dp'), may hold values from -6 to 6
Outputs:
- attended: bfloat16 [4096, 8192], P('ctx', 'dp')
- grad_query: bfloat16 [4096, 8192], P('ctx', 'dp')
- grad_key: bfloat16 [4096, 8192], P('ctx', 'dp')
- grad_value: bfloat16 [4096, 8192], P('ctx', 'dp')
- grad_gain: float32 [8192], P('dp')
The draws below stay inside these ranges and needn't reach their ends.
All inputs are finite; a program needn't handle non-finite values.
Results may differ from the reference program's by a relative error of at most 0.011.
Values sent between devices are 32-bit elements; how exact they have to be, the bound alone decides.
No kernel may reach another device: no remote copies, remote signals or barrier semaphores. Data moves between devices by JAX's collectives and lax.ppermute only.
A program may use at most 128 MiB of HBM per device.

```python
import math
import jax
import jax.numpy as jnp
from jax import lax

HEADS = 64
HEAD = 128
TOK_DEV = 512
BLOCK = 512
TOKEN_POSITIONS = 4096
FEATURES = 8192


def draw_log_decay(key, part):
    key = jax.random.fold_in(key, 11)
    segment_parts = jax.random.split(key, 8)
    fast_share = 0.5
    fast_heads = jax.random.uniform(segment_parts[0], (HEADS, 1)) < fast_share
    slow_rate = jax.random.uniform(segment_parts[1], (HEADS, 1), minval=0.15, maxval=0.6) / TOKEN_POSITIONS
    fast_rate = jnp.exp(jax.random.uniform(segment_parts[2], (HEADS, 1), minval=math.log(1.0 / 50.0), maxval=math.log(1.0 / 30.0)))
    baseline_rate = jnp.where(fast_heads, fast_rate, slow_rate)
    jaggedness = jax.random.uniform(segment_parts[3], (HEADS, TOKEN_POSITIONS), minval=0.5, maxval=1.5)
    device_factor = jnp.exp(jax.random.uniform(segment_parts[4], (TOKEN_POSITIONS // TOK_DEV,), minval=math.log(0.7), maxval=math.log(1.4)))
    dispersal_factor = jnp.repeat(device_factor, TOK_DEV)[None, :]
    midpoint_length = TOKEN_POSITIONS // 2
    leading_spike = jax.random.randint(segment_parts[5], (), 0, midpoint_length)
    trailing_spike = jax.random.randint(segment_parts[6], (), midpoint_length, TOKEN_POSITIONS)
    loss_values = jax.random.uniform(segment_parts[7], (HEADS, 2), minval=0.2, maxval=0.5)
    token_places = jnp.arange(TOKEN_POSITIONS)[None, :]
    spike_loss = jnp.where(token_places == leading_spike, jnp.log(1.0 - loss_values[:, 0:1]), 0.0)
    spike_loss = spike_loss + jnp.where(token_places == trailing_spike, jnp.log(1.0 - loss_values[:, 1:2]), 0.0)
    return (-baseline_rate * jaggedness * dispersal_factor + spike_loss).astype(jnp.float32)


def draw_value_in(key, part):
    key = jax.random.fold_in(key, 23)
    segment_parts = jax.random.split(key, 4)
    head_index = jnp.arange(FEATURES) // HEAD
    column_scale = jnp.exp(jax.random.uniform(segment_parts[0], (FEATURES,), minval=0.0, maxval=math.log(10.0)))
    column_scale = column_scale * jnp.exp(math.log(3.0) * head_index / max(HEADS - 1, 1)) / 4.0
    entries = jnp.clip(jax.random.normal(segment_parts[3], (TOKEN_POSITIONS, FEATURES)), -4.0, 4.0)
    return (entries * column_scale[None, :]).astype(jnp.bfloat16)


def shard_levels(stream_key, shape, pieces, smallest, high):
    def one(position, blocks):
        heights = jax.random.uniform(jax.random.fold_in(jax.random.fold_in(stream_key, 6), position), (blocks,), jnp.float32, smallest / len(pieces), high / len(pieces))
        return jnp.repeat(jnp.exp(heights), shape[position] // blocks).reshape((-1,) + (1,) * (len(shape) - position - 1))

    level = one(*pieces[0])
    for cut in pieces[1:]:
        level = level * one(*cut)
    return level


def noise(stream_key, extent, spread, limit, pieces=(), held_as=jnp.bfloat16):
    values = spread * jax.random.normal(stream_key, extent, jnp.float32)
    if pieces:
        values = values * shard_levels(stream_key, extent, pieces, -0.22, 0.18)
    return jnp.clip(values, -limit, limit).astype(held_as)


def setup_inputs(seed: int = 0) -> dict:
    key_list = jax.random.split(jax.random.key(seed), 7)
    return {
        "query_in": noise(key_list[0], (TOKEN_POSITIONS, FEATURES), 1.0, 6.0, ((0, 8), (1, 4))),
        "key_in": noise(key_list[1], (TOKEN_POSITIONS, FEATURES), 1.0, 6.0, ((0, 8), (1, 4))),
        "value_in": draw_value_in(jax.random.fold_in(key_list[6], 71), 0),
        "log_decay": draw_log_decay(jax.random.fold_in(key_list[6], 71), 0),
        "norm_gain": jnp.clip(1.0 + 0.15 * jax.random.normal(key_list[4], (FEATURES,), jnp.float32), 0.25, 1.75),
        "grad_out": noise(key_list[5], (TOKEN_POSITIONS, FEATURES), 1.0, 6.0, ((0, 8), (1, 4))),
    }


def decay_table(within):
    within_heads = within.T
    causal_mask = jnp.arange(BLOCK)[:, None] >= jnp.arange(BLOCK)[None, :]
    decay_gap = within_heads[:, :, None] - within_heads[:, None, :]
    return jnp.where(causal_mask, jnp.exp(jnp.where(causal_mask, decay_gap, 0.0)), 0.0)

def forward_block(carry_state, inputs):
    query_rows, key_rows, value_rows, within = inputs
    block_total = within[-1]
    decay_weights = decay_table(within)
    scores = jnp.einsum('thd,shd->hts', query_rows.astype(jnp.float32), key_rows.astype(jnp.float32))
    weighted = (scores * decay_weights).astype(jnp.bfloat16)
    local_mix = jnp.einsum('hts,shj->thj', weighted.astype(jnp.float32), value_rows.astype(jnp.float32))
    query_scaled = query_rows.astype(jnp.float32) * jnp.exp(within)[:, :, None]
    carried = jnp.einsum('thi,hij->thj', query_scaled, carry_state, precision=lax.Precision.HIGHEST)
    key_weighted = (key_rows.astype(jnp.float32) * jnp.exp(block_total[None, :] - within)[:, :, None]).astype(jnp.bfloat16)
    block_state = jnp.einsum('shi,shj->hij', key_weighted.astype(jnp.float32), value_rows.astype(jnp.float32))
    next_state = jnp.exp(block_total)[:, None, None] * carry_state + block_state
    return (next_state, (carried + local_mix, carry_state))

def backward_block(back_state, inputs):
    query_rows, key_rows, value_rows, within, start_state, grad_rows = inputs
    block_total = within[-1]
    decay_weights = decay_table(within)
    query_float = query_rows.astype(jnp.float32)
    key_float = key_rows.astype(jnp.float32)
    value_float = value_rows.astype(jnp.float32)
    grad_float = grad_rows.astype(jnp.float32)
    scores = jnp.einsum('thd,shd->hts', query_float, key_float)
    weighted = (scores * decay_weights).astype(jnp.bfloat16)
    grad_scores = jnp.einsum('thj,shj->hts', grad_float, value_float)
    grad_weighted = (grad_scores * decay_weights).astype(jnp.bfloat16).astype(jnp.float32)
    local_query = jnp.einsum('hts,shi->thi', grad_weighted, key_float)
    local_key = jnp.einsum('hts,thi->shi', grad_weighted, query_float)
    local_value = jnp.einsum('hts,thj->shj', weighted.astype(jnp.float32), grad_float)
    query_carried = jnp.exp(within)[:, :, None] * jnp.einsum('thj,hij->thi', grad_float, start_state, precision=lax.Precision.HIGHEST)
    tail_decay = jnp.exp(block_total[None, :] - within)[:, :, None]
    key_carried = tail_decay * jnp.einsum('shj,hij->shi', value_float, back_state, precision=lax.Precision.HIGHEST)
    value_carried = tail_decay * jnp.einsum('shi,hij->shj', key_float, back_state, precision=lax.Precision.HIGHEST)
    query_weighted = (query_float * jnp.exp(within)[:, :, None]).astype(jnp.bfloat16)
    block_back = jnp.einsum('uhi,uhj->hij', query_weighted.astype(jnp.float32), grad_float)
    next_back = jnp.exp(block_total)[:, None, None] * back_state + block_back
    outputs = ((query_carried + local_query).astype(jnp.bfloat16), (key_carried + local_key).astype(jnp.bfloat16), (value_carried + local_value).astype(jnp.bfloat16))
    return (next_back, outputs)

def reference(query_in, key_in, value_in, log_decay, norm_gain, grad_out):
    block_count = TOKEN_POSITIONS // BLOCK
    shaped = (block_count, BLOCK, HEADS, HEAD)
    query_rows = query_in.reshape(shaped)
    key_rows = key_in.reshape(shaped)
    value_rows = value_in.reshape(shaped)
    within = jnp.transpose(jnp.cumsum(log_decay.reshape(HEADS, block_count, BLOCK), axis=2), (1, 2, 0))
    zero_state = jnp.zeros((HEADS, HEAD, HEAD), jnp.float32)
    final_state, (raw_blocks, start_states) = lax.scan(forward_block, zero_state, (query_rows, key_rows, value_rows, within))
    raw_out = raw_blocks.reshape(TOKEN_POSITIONS, FEATURES)
    grad_float = grad_out.astype(jnp.float32)
    scaled_grad = grad_float * norm_gain
    square_sum = lax.optimization_barrier(jnp.sum(raw_out * raw_out, axis=1))
    cross_sum = lax.optimization_barrier(jnp.sum(scaled_grad * raw_out, axis=1))
    inv_rms = lax.rsqrt(square_sum / FEATURES + 1e-06)
    normed = raw_out * inv_rms[:, None]
    attended = (normed * norm_gain).astype(jnp.bfloat16)
    cubed = inv_rms * inv_rms * inv_rms
    grad_raw = (inv_rms[:, None] * scaled_grad - raw_out * cubed[:, None] * cross_sum[:, None] / FEATURES).astype(jnp.bfloat16)
    grad_gain = lax.optimization_barrier(jnp.sum(grad_float * normed, axis=0)) / math.sqrt(TOKEN_POSITIONS)
    grad_rows = grad_raw.reshape(shaped)
    final_back, (query_blocks, key_blocks, value_blocks) = lax.scan(backward_block, zero_state, (query_rows, key_rows, value_rows, within, start_states, grad_rows), reverse=True)
    grad_query = query_blocks.reshape(TOKEN_POSITIONS, FEATURES)
    grad_key = key_blocks.reshape(TOKEN_POSITIONS, FEATURES)
    grad_value = value_blocks.reshape(TOKEN_POSITIONS, FEATURES)
    return (attended, grad_query, grad_key, grad_value, grad_gain)
```

```python
import functools
import math

import jax
import jax.numpy as jnp
from jax import lax
from jax.experimental import pallas as pl
from jax.experimental.pallas import tpu as pltpu
from jax.sharding import PartitionSpec as P

BLOCK = 512
MIDDLE = BLOCK // 2
WIDTH = 128
EXTRA = 8
F32 = jnp.float32
BF16 = jnp.bfloat16
VMEM_LIMIT = 14 * 1024 * 1024

NN = (((1,), (0,)), ((), ()))
NT = (((1,), (1,)), ((), ()))
TN = (((0,), (0,)), ((), ()))
EARLY = slice(0, MIDDLE)
LATE = slice(MIDDLE, BLOCK)


def mul(left, right, form):
    return lax.dot_general(left, right, form, preferred_element_type=F32)


def twin(left, right, first, second):
    none = jnp.zeros(first.shape, BF16)
    above = jnp.concatenate([first.astype(BF16), none], axis=1)
    below = jnp.concatenate([none, second.astype(BF16)], axis=1)
    return mul(jnp.concatenate([left, right], axis=1), jnp.concatenate([above, below], axis=0), NN)


def iota(shape, axis):
    return lax.broadcasted_iota(jnp.int32, shape, axis)


def rows_of(i):
    return slice(i * WIDTH, (i + 1) * WIDTH)


def states_in(ref):
    return ref.shape[0] // WIDTH


def lanes(i):
    return slice(i * WIDTH, (i + 1) * WIDTH)


def pieces(value):
    first = value.astype(BF16)
    value = value - first.astype(F32)
    second = value.astype(BF16)
    return first, second, (value - second.astype(F32)).astype(BF16)


def apart(body):
    pl.when(lax.axis_index("ctx") >= 0)(body)


def first_head(side, chunk, heads, chunk_heads):
    half = lax.rem(lax.axis_index("ctx"), 2)
    if side:
        half = 1 - half
    return half * (heads // 2) + chunk * chunk_heads


def wide(head, i, count=1):
    return pl.ds(pl.multiple_of((head + i) * WIDTH, WIDTH), count * WIDTH)


def turned_to(column_ref, head):
    return pltpu.roll(column_ref[...], lax.rem(WIDTH - head, WIDTH), 1)


def write_decays(decay, row_ref, column_ref, grown_ref, tail_ref, log_ref):
    heads = decay.shape[0]
    upto = jnp.where(iota((WIDTH, WIDTH), 0) <= iota((WIDTH, WIDTH), 1), 1.0, 0.0).astype(BF16)
    carry = jnp.zeros((heads, 1), F32)
    blocks = []
    for block in range(BLOCK // WIDTH):
        total = carry
        for piece in pieces(decay[:, lanes(block)]):
            total = total + mul(piece, upto, NN)
        carry = total[:, WIDTH - 1 :]
        row_ref[:, lanes(block)] = total
        padded = jnp.concatenate([total, jnp.zeros((WIDTH - heads, WIDTH), F32)], axis=0)
        blocks.append(jnp.transpose(padded))
    mine = iota((heads, WIDTH), 1) == lax.axis_index("ctx")
    log_ref[...] = jnp.where(mine, jnp.broadcast_to(carry, (heads, WIDTH)), 0.0)
    within = jnp.concatenate(blocks, axis=0)
    column_ref[...] = within
    grown_ref[...] = jnp.exp(within)
    tail_ref[...] = jnp.exp(within[BLOCK - 1 :] - within)


def write_states(head, chunk, tail_ref, key_ref, value_ref, state_ref):
    tail = turned_to(tail_ref, head)
    count = states_in(state_ref)
    for i in range(count):
        at = lanes(chunk * count + i)
        weighted = (key_ref[:, at].astype(F32) * tail[:, i : i + 1]).astype(BF16)
        state_ref[rows_of(i)] = mul(weighted, value_ref[:, at], TN)


PARTS = 2


def row_part(n):
    return pl.ds(n * (BLOCK // PARTS), BLOCK // PARTS)


def pulled(source, target, sems, heads, side):
    copies = []
    at = wide(first_head(side, 0, heads, 0), 0, heads // 2)
    for part in range(PARTS):
        rows = row_part(part)
        copy = pltpu.make_async_copy(source.at[rows, at], target.at[rows], sems.at[part])
        copy.start()
        copies.append(copy)
    return copies


def flushed(held_refs, out_refs, sems, heads, side, chunk):
    copies = []
    for n, (held, out) in enumerate(zip(held_refs, out_refs)):
        count = held.shape[1] // WIDTH
        at = wide(first_head(side, chunk, heads, count), 0, count)
        for part in range(PARTS):
            rows = row_part(part)
            copy = pltpu.make_async_copy(held.at[rows], out.at[rows, at], sems.at[n, part])
            copy.start()
            copies.append(copy)
    return copies


def half_of(rows, side):
    count = rows.shape[0] // 2
    half = lax.rem(lax.axis_index("ctx"), 2)
    in_first = (half if side else 1 - half).astype(F32)
    return in_first * rows[:count] + (1.0 - in_first) * rows[count:]


def first_kernel(
    decay_in, key_in, value_in, row_ref, column_ref, grown_ref, tail_ref, log_ref, key_ref, value_ref,
    own_key_ref, own_value_ref, state_ref, decay_ref, decay_sem, sems, *, heads
):
    chunk_heads = states_in(state_ref)
    decay_copy = pltpu.make_async_copy(decay_in, decay_ref, decay_sem.at[0])
    decay_copy.start()
    copies = []
    for side, targets in ((1, (key_ref, value_ref)), (0, (own_key_ref, own_value_ref))):
        for chunk in range(2 if side else 1):
            count = chunk_heads if side else heads // 2
            at = wide(first_head(side, chunk, heads, count), 0, count)
            here = slice(chunk * count * WIDTH, (chunk + 1) * count * WIDTH)
            for source, target in zip((key_in, value_in), targets):
                copy = pltpu.make_async_copy(source.at[:, at], target.at[:, here], sems.at[len(copies)])
                copy.start()
                copies.append(copy)
    decay_copy.wait()
    write_decays(decay_ref[...], row_ref, column_ref, grown_ref, tail_ref, log_ref)
    for copy in copies[:2]:
        copy.wait()
    write_states(first_head(1, 0, heads, 0), 0, tail_ref, key_ref, value_ref, state_ref)
    for copy in copies[2:]:
        copy.wait()


def state_kernel(tail_ref, key_ref, value_ref, *refs, heads, side, chunk, load_side):
    copies = []
    if load_side is None:
        state_ref = refs[-1]
    else:
        state_ref, target, sems = refs[-3:]
        copies = pulled(refs[0], target, sems, heads, load_side)
    head = first_head(side, chunk, heads, states_in(state_ref))

    @apart
    def _():
        write_states(head, chunk, tail_ref, key_ref, value_ref, state_ref)

    for copy in copies:
        copy.wait()


TURNED_STRIPS = ((slice(0, WIDTH), slice(0, MIDDLE)), (slice(WIDTH, MIDDLE), slice(WIDTH, MIDDLE)))


def shifted(part, block):
    return slice(part.start + block * MIDDLE, part.stop + block * MIDDLE)


def local_kernel(
    row_ref, column_ref, grown_ref, query_ref, key_ref, value_ref, *refs, heads, side, chunk, loading
):
    copies = []
    if loading:
        out_ref, query_out, turned_out, state_ref, weighted_ref, decay_ref, *targets, sems = refs[-9:]
        for n in range(2):
            copies += pulled(refs[0], targets[n], sems.at[n], heads, n)
    else:
        out_ref, query_out, turned_out, state_ref, weighted_ref, decay_ref = refs[-6:]
    chunk_heads = state_ref.shape[0]

    @apart
    def _():
        head = first_head(side, chunk, heads, chunk_heads)
        column = turned_to(column_ref, head)
        grown = turned_to(grown_ref, head)
        middle = column[MIDDLE - 1 : MIDDLE]
        upto = jnp.exp(jnp.minimum(middle - column[EARLY], 0.0))
        since = jnp.exp(jnp.minimum(column[LATE] - middle, 0.0))
        seen = (
            iota((WIDTH, MIDDLE), 1) >= iota((WIDTH, MIDDLE), 0),
            iota((WIDTH, WIDTH), 1) >= iota((WIDTH, WIDTH), 0),
        )

        def spread(i):
            at = lanes(chunk * chunk_heads + i)
            row = row_ref[pl.ds(head + i, 1), :]
            for block in range(2):
                for mask, (here, there) in zip(seen, TURNED_STRIPS):
                    rows, other = shifted(here, block), shifted(there, block)
                    gap = row[:, other] - column[rows, i : i + 1]
                    decay = jnp.where(mask, jnp.exp(jnp.minimum(gap, 0.0)), 0.0)
                    scores = mul(key_ref[rows, at], query_ref[other, at], NT)
                    weighted_ref[i, rows, there] = (scores * decay).astype(BF16)
                    decay_ref[i, rows, there] = decay.astype(BF16)

        def gather(i):
            at = lanes(chunk * chunk_heads + i)
            weighted_query = query_ref[:, at].astype(F32) * grown[:, i : i + 1]
            query_out[:, lanes(i)] = weighted_query.astype(BF16)
            turned_out[lanes(i), :] = jnp.transpose(weighted_query).astype(BF16)
            key = (key_ref[EARLY, at].astype(F32) * upto[:, i : i + 1]).astype(BF16)
            state = mul(key, value_ref[EARLY, at], TN).astype(BF16)
            state_ref[i] = state
            query = (query_ref[LATE, at].astype(F32) * since[:, i : i + 1]).astype(BF16)
            for block in range(2):
                first, second = (shifted(here, block) for here, _ in TURNED_STRIPS)
                both = slice(first.start, second.stop)
                terms = (
                    mul(weighted_ref[i, first, :WIDTH], value_ref[first, at], TN),
                    mul(weighted_ref[i, both, WIDTH:], value_ref[both, at], TN),
                )
                for rows, term in zip((first, second), terms):
                    if block:
                        term = term + mul(query[rows.start - MIDDLE : rows.stop - MIDDLE], state, NN)
                    out_ref[rows, lanes(i)] = term.astype(BF16)

        spread(0)
        for i in range(chunk_heads):
            if i + 1 < chunk_heads:
                spread(i + 1)
            gather(i)

    for copy in copies:
        copy.wait()


def raw_kernel(local_ref, query_ref, grad_ref, gain_ref, start_ref, *refs, heads, side, chunk, first, last):
    raw_ref, sums_ref = refs[-2:]
    count = states_in(start_ref)
    head = first_head(side, chunk, heads, count)
    squares = jnp.zeros((BLOCK, WIDTH), F32) if first else refs[0][0]
    crosses = jnp.zeros((BLOCK, WIDTH), F32) if first else refs[0][1]
    both = None
    for i in range(count):
        at = lanes(chunk * count + i)
        if i % 2:
            raw = both[:, WIDTH:]
        elif i + 1 < count:
            both = twin(
                query_ref[:, lanes(i)], query_ref[:, lanes(i + 1)], start_ref[rows_of(i)], start_ref[rows_of(i + 1)]
            )
            raw = both[:, :WIDTH]
        else:
            raw = mul(query_ref[:, lanes(i)], start_ref[rows_of(i)].astype(BF16), NN)
        raw = raw + local_ref[:, lanes(i)].astype(F32)
        raw_ref[:, lanes(i)] = raw.astype(BF16)
        squares = squares + raw * raw
        crosses = crosses + grad_ref[:, at].astype(F32) * gain_ref[0:1, wide(head, i)] * raw
    if last:
        sums_ref[0:1, :] = jnp.sum(jnp.transpose(squares), axis=0, keepdims=True)
        sums_ref[1:2, :] = jnp.sum(jnp.transpose(crosses), axis=0, keepdims=True)
    else:
        sums_ref[0] = squares
        sums_ref[1] = crosses


def back_kernel(turned_ref, raw_ref, grad_ref, gain_ref, sums_ref, *refs, heads, side, chunk, first, features):
    if first:
        out_ref, state_ref, norm_ref = refs[-3:]
        total = sums_ref[...] + refs[0][...]
        inverse = lax.rsqrt(total[0:1] / features + 1e-06)
        cross = inverse * inverse * inverse * total[1:2] / features
        norm_ref[0] = jnp.transpose(jnp.broadcast_to(inverse, (WIDTH, BLOCK)))
        norm_ref[1] = jnp.transpose(jnp.broadcast_to(cross, (WIDTH, BLOCK)))
    else:
        out_ref, state_ref = refs[-2:]
        norm_ref = sums_ref
    count = states_in(state_ref)
    head = first_head(side, chunk, heads, count)
    state_ref[count * WIDTH :] = jnp.zeros((EXTRA, WIDTH), F32)
    for i in range(count):
        raw = raw_ref[:, lanes(i)].astype(F32)
        cotangent = grad_ref[:, lanes(chunk * count + i)].astype(F32)
        grad = norm_ref[0] * (cotangent * gain_ref[0:1, wide(head, i)]) - raw * norm_ref[1]
        grad = grad.astype(BF16)
        out_ref[:, lanes(i)] = grad
        state_ref[rows_of(i)] = mul(turned_ref[lanes(i), :], grad, NN)
        terms = jnp.sum(cotangent * (raw * norm_ref[0]), axis=0, keepdims=True)
        state_ref[count * WIDTH + i : count * WIDTH + i + 1] = terms


def ready_kernel(column_ref, tail_ref, query_ref, key_ref, value_ref, *refs, heads, side, chunk):
    key_out, value_out, since_out = refs[-3:]
    chunk_heads = key_out.shape[1] // WIDTH
    head = first_head(side, chunk, heads, chunk_heads)
    column = turned_to(column_ref, head)
    tail = turned_to(tail_ref, head)
    since = jnp.exp(jnp.minimum(column[LATE] - column[MIDDLE - 1 : MIDDLE], 0.0))
    for i in range(chunk_heads):
        at = lanes(chunk * chunk_heads + i)
        query = query_ref[LATE, at].astype(F32) * since[:, i : i + 1]
        since_out[lanes(i), :] = jnp.transpose(query).astype(BF16)
        key_out[:, lanes(i)] = (key_ref[:, at].astype(F32) * tail[:, i : i + 1]).astype(BF16)
        value_out[:, lanes(i)] = (value_ref[:, at].astype(F32) * tail[:, i : i + 1]).astype(BF16)


def grad_kernel(
    column_ref, grown_ref, query_ref, key_ref, value_ref, grad_ref, raw_ref, gain_ref, norm_ref,
    start_ref, middle_ref, since_ref, weighted_ref, decay_ref, *refs, heads, side, chunk, done
):
    chunk_heads = weighted_ref.shape[0]
    head = first_head(side, chunk, heads, chunk_heads)
    if done is not None:
        query_all, attended_all, query_out, attended_out, key_out, value_out, spread_ref, sems = refs[-8:]
        copies = flushed(refs[:2], (query_all, attended_all), sems, heads, *done)
    else:
        query_out, attended_out, key_out, value_out, spread_ref = refs[-5:]
        copies = []
    @apart
    def _():
        column = turned_to(column_ref, head)
        grown = turned_to(grown_ref, head)
        middle = column[MIDDLE - 1 : MIDDLE]
        upto = jnp.exp(jnp.minimum(middle - column[EARLY], 0.0))
        since = jnp.exp(jnp.minimum(column[LATE] - middle, 0.0))

        def spread(i):
            at = lanes(chunk * chunk_heads + i)
            here = lanes(i)
            for block in range(2):
                for mine, others in TURNED_STRIPS:
                    rows, other = shifted(mine, block), shifted(others, block)
                    grad_scores = mul(value_ref[rows, at], grad_ref[other, here], NT)
                    grad_weighted = grad_scores * decay_ref[i, rows, others].astype(F32)
                    spread_ref[i % 2, rows, others] = grad_weighted.astype(BF16)

        def gather(i):
            at = lanes(chunk * chunk_heads + i)
            here = lanes(i)
            normed = raw_ref[:, here].astype(F32) * norm_ref[0]
            attended_out[:, here] = (normed * gain_ref[0:1, wide(head, i)]).astype(BF16)
            state = start_ref[rows_of(i)]
            half_state = grown[MIDDLE - 1 : MIDDLE, i : i + 1] * state + middle_ref[i].astype(F32)
            back = mul(since_ref[here, :], grad_ref[LATE, here], NN)
            ends = twin(value_ref[EARLY, at], key_ref[EARLY, at], jnp.transpose(back), back)
            carried = twin(
                grad_ref[EARLY, here], grad_ref[LATE, here], jnp.transpose(state), jnp.transpose(half_state)
            )
            for block in range(2):
                for mine, others in TURNED_STRIPS:
                    rows, other = shifted(mine, block), shifted(others, block)
                    grad_weighted = spread_ref[i % 2, rows, others]
                    grad_value = mul(weighted_ref[i, rows, others], grad_ref[other, here], NN)
                    grad_key = mul(grad_weighted, query_ref[other, at], NN)
                    if not block:
                        factor = upto[rows, i : i + 1]
                        grad_key = grad_key + factor * ends[rows, :WIDTH]
                        grad_value = grad_value + factor * ends[rows, WIDTH:]
                    key_out[rows, here] = grad_key.astype(BF16)
                    value_out[rows, here] = grad_value.astype(BF16)
                first, second = (shifted(mine, block) for mine, _ in TURNED_STRIPS)
                both = slice(first.start, second.stop)
                terms = (
                    mul(spread_ref[i % 2, first, :WIDTH], key_ref[first, at], TN),
                    mul(spread_ref[i % 2, both, WIDTH:], key_ref[both, at], TN),
                )
                for rows, term in zip((first, second), terms):
                    if block:
                        mine = slice(rows.start - MIDDLE, rows.stop - MIDDLE)
                        factor = since[mine, i : i + 1]
                    else:
                        mine = rows
                        factor = grown[rows, i : i + 1]
                    query_out[rows, here] = (term + factor * carried[mine, lanes(block)]).astype(BF16)

        spread(0)
        for i in range(chunk_heads):
            if i + 1 < chunk_heads:
                spread(i + 1)
            gather(i)

    for copy in copies:
        copy.wait()


def end_kernel(*refs, heads, spots, done, rest, scale):
    groups = [refs[5 * n : 5 * n + 5] for n in range(len(spots))]
    refs = refs[5 * len(spots) :]
    chunk_heads = states_in(groups[0][4])
    copies = []
    if done is not None:
        query_all, attended_all, key_all, value_all, key_out, value_out, sems, own_sems = refs[-8:]
        copies += flushed(refs[:2], (query_all, attended_all), sems, heads, *done)
    else:
        key_all, value_all, gain_out, key_out, value_out, own_sems = refs[-6:]
    size = chunk_heads
    for n, (key_ref, value_ref, key_part, value_part, end_ref) in enumerate(groups):
        head = first_head(*spots[n], heads, chunk_heads)
        for piece in range(chunk_heads // size):

            @apart
            def _():
                for i in range(piece * size, (piece + 1) * size):
                    here = lanes(i)
                    end = end_ref[rows_of(i)].astype(BF16)
                    key_term = mul(value_ref[:, here], end, NT)
                    key_out[n, :, here] = (key_term + key_part[:, here].astype(F32)).astype(BF16)
                    value_term = mul(key_ref[:, here], end, NN)
                    value_out[n, :, here] = (value_term + value_part[:, here].astype(F32)).astype(BF16)

            held = (key_out.at[n], value_out.at[n])
            copies += flushed(held, (key_all, value_all), own_sems.at[n], heads, *spots[n])
    if done is None:

        @apart
        def _():
            sources = [(spot, group[4]) for spot, group in zip(spots, groups)] + list(zip(rest, refs))
            for spot, source in sources:
                head = first_head(*spot, heads, chunk_heads)
                for i in range(chunk_heads):
                    at = chunk_heads * WIDTH + i
                    gain_out[pl.ds(head + i, 1), :] = source[at : at + 1] * scale

    for copy in copies:
        copy.wait()


def sum_kernel(left_ref, right_ref, *refs):
    refs[-1][...] = left_ref[...] + right_ref[...]


def pass_kernel(left_ref, right_ref, state_ref, *refs):
    refs[-2][...] = left_ref[...] + right_ref[...]
    refs[-1][...] = state_ref[...]


def blend_kernel(factor_ref, *refs, rows, first, inputs, outputs, plain):
    ins, outs = refs[:inputs], refs[len(refs) - outputs :]
    for which, out_ref in enumerate(outs):
        count = states_in(out_ref)
        for i in range(count):
            total = None
            for source, row in zip(ins, rows[which]):
                if row is None:
                    continue
                term = factor_ref[row, first + i : first + i + 1, :] * source[rows_of(i)]
                total = term if total is None else total + term
            out_ref[rows_of(i)] = total
        if out_ref.shape[0] > count * WIDTH:
            below = slice(count * WIDTH, None)
            out_ref[below] = ins[plain[0]][below] + ins[plain[1]][below]


def swap(value, axis, bit):
    return lax.ppermute(value, axis, [(i, i ^ bit) for i in range(lax.axis_size(axis))])


def butterfly(value, axis):
    bit = 1
    while bit < lax.axis_size(axis):
        value = value + swap(value, axis, bit)
        bit *= 2
    return value


def pair_bits(count):
    in_order = [2 << n for n in range((count // 2).bit_length() - 1)]
    return [(bit, other) for bit, other in zip(in_order, in_order[::-1] if count == 8 else in_order)]


def factor_kernel(*refs, parts, count, backward):
    out_ref = refs[-1]
    logs = refs[0][...]
    for ref in refs[1:parts]:
        logs = logs + ref[...]
    logs = half_of(logs, 0)
    device = lax.axis_index("ctx")
    half = lax.rem(device, 2)
    in_first = (1 - half).astype(F32)
    place = iota(logs.shape, 1)
    mine = device
    if backward:
        place = count - 1 - place
        mine = count - 1 - device
    late = lax.rem(mine, 2).astype(F32)
    pair = mine // 2
    one = jnp.ones_like(logs)

    def choose(condition, yes, no):
        chosen = condition.astype(F32) if condition.dtype == jnp.bool_ else condition
        return chosen * yes + (1.0 - chosen) * no

    def devices(low, high):
        inside = (place >= low) & (place < high)
        total = jnp.sum(jnp.where(inside, logs, 0.0), axis=1, keepdims=True)
        return jnp.exp(jnp.broadcast_to(total, logs.shape))

    def span(low, high):
        return devices(2 * low, 2 * high)

    early_decay = devices(2 * pair, 2 * pair + 1)
    late_decay = devices(2 * pair + 1, 2 * pair + 2)
    rows = [choose(late, one, late_decay), choose(late, late_decay, one)]
    sent = one
    stages = []
    for bit, _ in pair_bits(count):
        size = bit // 2
        low = pair // size * size
        odd = lax.rem(pair // size, 2)
        other = low + size - 2 * odd * size
        later = odd.astype(F32)
        stages.append((
            later * span(low, pair),
            choose(later, one, span(other, other + size)),
            choose(later, span(low, low + size), one),
        ))
    if count == 8:
        high, low = pair // 2, lax.rem(pair, 2)
        below = high.astype(F32)
        sent = in_first * one + (1.0 - in_first) * span(pair + 1, 2 * high + 2)
        across = [
            (below * span(2 * high, pair), (1.0 - low.astype(F32)) * one, below * span(pair, 2 * high + 1)),
            (one, 0.0 * one, 0.0 * one),
        ]
        stages = [
            tuple(in_first * x + (1.0 - in_first) * y for x, y in zip(plain, other))
            for plain, other in zip(stages, across)
        ]
    rows += [sent * rows[0], sent * rows[1]]
    for _, keep, add in stages:
        rows += [keep, add]
    own_factor = choose(late, early_decay, one)
    given_factor = choose(late, one, early_decay)
    rows += [own_factor * take for take, _, _ in stages] + [late * one]
    rows += [given_factor * take for take, _, _ in stages] + [(1.0 - late) * one]
    for n, row in enumerate(rows):
        out_ref[n] = row


def on_device(query_in, key_in, value_in, log_decay, norm_gain, grad_out):
    heads = log_decay.shape[0]
    half_heads = heads // 2
    chunks = 2
    chunk_heads = half_heads // chunks
    shards = lax.axis_size("dp")
    count = lax.axis_size("ctx")
    features = heads * WIDTH * shards
    positions = BLOCK * count
    gain = norm_gain.reshape(1, -1)
    bits = pair_bits(count)
    stages = len(bits)

    vmem_spec = pl.BlockSpec(memory_space=pltpu.VMEM)
    any_spec = pl.BlockSpec(memory_space=pl.ANY)

    def held(shape, dtype=BF16):
        return pltpu.VMEM(shape, dtype)

    part = (BLOCK, chunk_heads * WIDTH)
    half_shape = (BLOCK, half_heads * WIDTH)
    state_shape = (chunk_heads * WIDTH, WIDTH)
    long_shape = (chunk_heads * WIDTH + EXTRA, WIDTH)
    column_shape = (BLOCK, WIDTH)
    table_shape = (chunk_heads, BLOCK, MIDDLE)
    result = pltpu.HBM((BLOCK, heads * WIDTH), BF16)

    def call(body, name, ins, outs, far=(), scratch=(), after=(), into=()):
        near = [pltpu.with_memory_space_constraint(value, pltpu.VMEM) for value in ins]
        far = [pltpu.with_memory_space_constraint(value, pltpu.HBM) for value in list(far) + list(into)]
        aliases = {len(near) + len(far) - len(into) + n: n for n in range(len(into))}
        extra = far + list(after)
        return pl.pallas_call(
            body,
            name=name,
            in_specs=[vmem_spec] * len(near) + [any_spec] * len(extra),
            out_specs=[any_spec if out is result else vmem_spec for out in outs],
            out_shape=list(outs),
            scratch_shapes=list(scratch),
            input_output_aliases=aliases,
            compiler_params=pltpu.CompilerParams(vmem_limit_bytes=VMEM_LIMIT),
            cost_estimate=pl.CostEstimate(flops=10000, bytes_accessed=1024, transcendentals=0),
        )(*near, *extra)

    class Scan:
        def __init__(self, shape, opened):
            self.shape = held(shape, F32)
            self.opened = [held(shape, F32) for shape in opened]
            self.arrived = [[] for _ in range(chunks)]
            self.received, self.own, self.message = ({}, {}, {})

        def blend(self, chunk, factors, ins, rows, plain, after, shape=None):
            body = functools.partial(
                blend_kernel, rows=rows, first=chunk * chunk_heads, inputs=len(ins), outputs=len(rows),
                plain=plain,
            )
            return call(body, "blend", [factors, *ins], [shape or self.shape] * len(rows), after=after)

        def send(self, chunk, state):
            self.received[chunk] = swap(state, "ctx", 1)

        def forward(self, chunk, message, sent=None):
            plain, other = bits[len(self.arrived[chunk])]
            pairs = [(i, i ^ (other if i % 2 else plain)) for i in range(count)]
            self.message[chunk] = message
            self.arrived[chunk].append(lax.ppermute(message if sent is None else sent, "ctx", pairs))

        def open(self, chunk, factors, state, after=()):
            self.own[chunk] = state
            ins = [state, self.received[chunk]]
            message, sent = self.blend(chunk, factors, ins, [[0, 1], [2, 3]], (0, 1), after, self.opened[chunk])
            self.message[chunk] = message
            if stages:
                self.forward(chunk, message, sent)
            return message

        def step(self, chunk, factors, after=()):
            at = 2 + 2 * len(self.arrived[chunk])
            ins = [self.message[chunk], self.arrived[chunk][-1]]
            message = self.blend(chunk, factors, ins, [[at, at + 1]], (0, 1), after)[0]
            self.forward(chunk, message)
            return message

        def close(self, chunk, factors, after=()):
            at = 4 + 2 * stages
            ins = self.arrived[chunk] + [self.received[chunk], self.own[chunk], self.message[chunk]]
            own_rows = list(range(at, at + stages)) + [at + stages, None, None]
            at += stages + 1
            given_rows = list(range(at, at + stages)) + [None, at + stages, None]
            plain = (stages - 1, stages + 2) if stages else (0, 1)
            own, given = self.blend(chunk, factors, ins, [own_rows, given_rows], plain, after)
            return own, swap(given, "ctx", 1), given

    own, other = 0, 1
    order = [(side, chunk) for side in (own, other) for chunk in range(chunks)]
    spots = {(side, chunk): dict(heads=heads, side=side, chunk=chunk) for side, chunk in order}
    ahead = Scan(state_shape, [state_shape] * chunks)
    behind = Scan(long_shape, [long_shape] * chunks)
    factor_rows = 6 + 4 * stages

    def factors_of(logs, backward, after=()):
        body = functools.partial(factor_kernel, parts=len(logs), count=count, backward=backward)
        return call(body, "factors", logs, [held((factor_rows, half_heads, WIDTH), F32)], after=after)[0]

    def total(left, right, after):
        return call(sum_kernel, "sums", [left, right], [held(left.shape, F32)], after=after)[0]

    keys, values, queries, cotangents, states = ({}, {}, {}, {}, {})
    pull_sems = pltpu.SemaphoreType.DMA((2, PARTS))
    (row_values, column_values, grown, tails, placed, keys[other], values[other], keys[own], values[own],
     states[other, 0]) = call(
        functools.partial(first_kernel, heads=heads), "first_state", [],
        [held((heads, BLOCK), F32)] + [held(column_shape, F32)] * 3
        + [held((heads, WIDTH), F32)] + [held(half_shape)] * 4 + [held(state_shape, F32)],
        [log_decay, key_in, value_in],
        [pltpu.VMEM((heads, BLOCK), F32), pltpu.SemaphoreType.DMA((1,)), pltpu.SemaphoreType.DMA((6,))],
    )

    def state_call(side, chunk, load_side, after):
        loads = [] if load_side is None else [query_in]
        states[side, chunk], *loaded = call(
            functools.partial(state_kernel, load_side=load_side, **spots[side, chunk]),
            "local_state", [tails, keys[side], values[side]],
            [held(state_shape, F32)] + [held(half_shape) for _ in loads], loads,
            [pltpu.SemaphoreType.DMA((PARTS,)) for _ in loads], after,
        )
        for array in loaded:
            queries[load_side] = array
        return (states[side, chunk],)

    reach = [2] if count == 8 else [2 << n for n in range(stages)]
    logs = placed
    there = swap(logs, "ctx", reach[0]) if reach else None
    ahead.send(0, states[other, 0])
    last = state_call(other, 1, own, (states[other, 0],))
    last = state_call(own, 0, None, last)
    for bit in reach[1:]:
        logs = total(logs, there, last)
        there = swap(logs, "ctx", bit)
    sent = states[other, 1]
    if reach:
        logs, sent = call(
            pass_kernel, "logs", [logs, there, sent], [held(logs.shape, F32), held(state_shape, F32)], after=last
        )
        last = (logs,)
    ahead.send(1, sent)
    all_logs = [logs, swap(logs, "ctx", 1)]
    last = state_call(own, 1, other, last)
    factors = factors_of(all_logs, False, last)
    last = (ahead.open(0, factors, states[own, 0]),)
    last = (ahead.open(1, factors, states[own, 1], last),)

    locals_, ready = ({}, {})

    def local_call(side, chunk, after):
        loading = not cotangents
        outs = call(
            functools.partial(local_kernel, loading=loading, **spots[side, chunk]), "local_mix",
            [row_values, column_values, grown, queries[side], keys[side], values[side]],
            [held(part), held(part), held((chunk_heads * WIDTH, BLOCK)), held((chunk_heads, WIDTH, WIDTH)),
             held(table_shape), held(table_shape)] + [held(half_shape)] * (2 * loading),
            [grad_out] * loading, [pull_sems] * loading, after,
        )
        if loading:
            cotangents[own], cotangents[other] = outs[6:]
        locals_[side, chunk] = outs[:6]
        return (outs[0],)

    def ready_call(side, chunk, after):
        ready[side, chunk] = call(
            functools.partial(ready_kernel, **spots[side, chunk]), "weighted",
            [column_values, tails, queries[side], keys[side], values[side]],
            [held(part), held(part), held((chunk_heads * WIDTH, MIDDLE))], after=after,
        )
        return (ready[side, chunk][0],)

    to_mix, to_ready = list(order), list(order)
    last = local_call(*to_mix.pop(0), last)
    for stage in range(1, stages):
        for chunk in range(chunks):
            last = (ahead.step(chunk, factors, last),)
            if to_mix:
                last = local_call(*to_mix.pop(0), last)
    back_factors = factors_of(all_logs, True, last)
    last = (back_factors,)
    starts, raws = ({}, {})
    sums = []

    def raw_call(side, chunk, after):
        nonlocal sums
        final = (side, chunk) == order[-1]
        raws[side, chunk], sums_out = call(
            functools.partial(raw_kernel, first=not sums, last=final, **spots[side, chunk]), "raw_out",
            [*locals_[side, chunk][:2], cotangents[side], gain, starts[side, chunk]] + sums,
            [held(part), held((2, BLOCK) if final else (2, BLOCK, WIDTH), F32)], after=after,
        )
        sums = [sums_out]
        return (sums_out,)

    for chunk in range(chunks):
        starts[own, chunk], starts[other, chunk], given = ahead.close(chunk, factors, last)
        last = raw_call(own, chunk, (given,))
        while to_mix:
            last = local_call(*to_mix.pop(0), last)
    for chunk in range(chunks):
        last = raw_call(other, chunk, last)
    sums = sums[0]

    arrived = None
    bit = 1
    while bit < shards:
        if arrived is not None:
            sums = total(sums, arrived, last)
            last = (sums,)
        arrived = swap(sums, "dp", bit)
        for _ in range(2):
            if to_ready:
                last = ready_call(*to_ready.pop(0), last)
        bit *= 2
    if arrived is None:
        arrived = jnp.zeros_like(sums)

    grads = {}
    norms = None
    for side, chunk in [(other, chunk) for chunk in range(chunks)] + [(own, chunk) for chunk in range(chunks)]:
        first = norms is None
        grads[side, chunk], state, *more = call(
            functools.partial(back_kernel, features=features, first=first, **spots[side, chunk]), "grad_raw",
            [locals_[side, chunk][2], raws[side, chunk], cotangents[side], gain]
            + ([sums, arrived] if first else [norms]),
            [held(part), held(long_shape, F32)] + [held((2, BLOCK, WIDTH), F32)] * first, after=last,
        )
        norms = more[0] if first else norms
        last = (state,)
        if side == other:
            behind.send(chunk, state)
        else:
            last = (behind.open(chunk, back_factors, state),)

    parts = {}
    kept = None
    results = []

    def grad_call(side, chunk, after):
        nonlocal kept, results
        flush = kept is not None
        outs = call(
            functools.partial(grad_kernel, done=kept[0] if flush else None, **spots[side, chunk]), "local_grads",
            [column_values, grown, queries[side], keys[side], values[side], grads[side, chunk],
             raws[side, chunk], gain, norms, starts[side, chunk], locals_[side, chunk][3], ready[side, chunk][2], *locals_[side, chunk][4:],
             *(kept[1] if flush else [])],
            [result] * (2 * flush) + [held(part)] * 4, (),
            [pltpu.VMEM((2, BLOCK, MIDDLE), BF16)] + [pull_sems] * flush, after, results,
        )
        if flush:
            results = outs[:2]
        kept = ((side, chunk), outs[-4:-2])
        parts[side, chunk] = outs[-2:]
        return (outs[-1],)

    to_grad = list(order)
    last = grad_call(*to_grad.pop(0), last)
    for stage in range(1, stages):
        for chunk in range(chunks):
            if to_ready:
                last = ready_call(*to_ready.pop(0), last)
            last = (behind.step(chunk, back_factors, last),)
            if to_grad:
                last = grad_call(*to_grad.pop(0), last)
    while to_ready:
        last = ready_call(*to_ready.pop(0), last)
    ends = {}
    for chunk in range(chunks):
        if chunk:
            while to_grad:
                last = grad_call(*to_grad.pop(0), last)
        ends[own, chunk], ends[other, chunk], given = behind.close(chunk, back_factors, last)
        last = (given,)

    def end_call(places, held_ins, done, rest, outs, after, into):
        groups = [[*ready[place][:2], *parts[place], ends[place]] for place in places]
        body = functools.partial(
            end_kernel, heads=heads, spots=places, done=done, rest=rest, scale=1.0 / math.sqrt(positions)
        )
        room = pltpu.VMEM((len(places), *part), BF16)
        return call(
            body, "carried_grads", sum(groups, []) + held_ins, outs, (),
            [room, room, *([pull_sems] * (done is not None)), pltpu.SemaphoreType.DMA((len(places), 2, 2))],
            after, into,
        )

    early = [(own, 0), (other, 0)]
    query_result, attended, *into = end_call(early, list(kept[1]), kept[0], [], [result] * 4, last, results)
    key_result, value_result, gain_result = end_call(
        [(own, 1), (other, 1)], [ends[place] for place in early], None, early,
        [result, result, jax.ShapeDtypeStruct((heads, WIDTH), F32)], (), into,
    )
    return attended, query_result, key_result, value_result, gain_result.reshape(-1)


def solution(mesh):
    in_specs = (
        P("ctx", "dp"),
        P("ctx", "dp"),
        P("ctx", "dp"),
        P("dp", "ctx"),
        P("dp"),
        P("ctx", "dp"),
    )
    out_specs = (P("ctx", "dp"), P("ctx", "dp"), P("ctx", "dp"), P("ctx", "dp"), P("dp"))
    return jax.shard_map(
        on_device, mesh=mesh, in_specs=in_specs, out_specs=out_specs, check_vma=False
    )
```
